256 devices in a mesh: leaf: 16 (over x, y_hi, core), wide: 16 (over z, y_lo).
Axes of the slice: x: 4, y: 4 (y_hi: 2, y_lo: 2; y = y_hi * 2 + y_lo), z: 8, core: 2. Of those that a mesh axis runs over, the one named last changes fastest.
Arguments:
- source: bfloat16 [4, 16, 16, 256, 1024], P(None, 'leaf', 'wide'), may hold values from -6 to 6
- row_factors: bfloat16 [4, 4, 16, 16, 256, 512], P(None, None, 'leaf', 'wide'), may hold values from -0.25 to 0.25
- column_factors: bfloat16 [4, 4, 16, 16, 256, 512], P(None, None, 'leaf', 'wide'), may hold values from -0.25 to 0.25
Outputs:
- result: bfloat16 [4, 16, 16, 256, 1024], P(None, 'leaf', 'wide')
The draws below stay inside these ranges and needn't reach their ends.
All inputs are finite; a program needn't handle non-finite values.
Results may differ from the reference program's by a relative error of at most 0.015.
Values may be sent and summed in bfloat16 or wider, within the bound.
No kernel may reach another device: no remote copies, remote signals or barrier semaphores. Data moves between devices by JAX's collectives and lax.ppermute only.
A program may use at most 64 MiB of HBM per device.

```python
import jax
import jax.numpy as jnp

RANK = 256
RHS = 1024
BLK_DEV = 4
LEVELS = 4
LEAVES = 16
STRIPS = 16


def block_scale(rng, extent, shards, low, largest):
    def one(axis_at, blocks):
        heights = jax.random.uniform(jax.random.fold_in(jax.random.fold_in(rng, 6), axis_at), (blocks,), jnp.float32, low / len(shards), largest / len(shards))
        return jnp.repeat(jnp.exp(heights), extent[axis_at] // blocks).reshape((-1,) + (1,) * (len(extent) - axis_at - 1))

    gain = one(*shards[0])
    for cut in shards[1:]:
        gain = gain * one(*cut)
    return gain


def bell_draw(key, dims, deviation, bound, pieces=(), kind=jnp.bfloat16):
    factor_of = block_scale(key, dims, pieces, -0.22, 0.18) if pieces else 1.0
    array = jax.random.normal(key, dims, jnp.float32) * deviation * factor_of
    return jnp.minimum(jnp.maximum(array, -bound), bound).astype(kind)


def setup_inputs(seed: int = 0) -> dict:
    seeds = jax.random.split(jax.random.key(seed), 4)
    source = bell_draw(seeds[0], (BLK_DEV, LEAVES, STRIPS, RANK, RHS), 1.0, 6.0, ((1, 16), (2, 16)))
    row_factors = bell_draw(seeds[1], (LEVELS, BLK_DEV, LEAVES, STRIPS, RANK, 2 * RANK), (2 * RANK) ** -0.5, 0.25, ((2, 16), (3, 16)))
    column_factors = bell_draw(seeds[2], (LEVELS, BLK_DEV, LEAVES, STRIPS, RANK, 2 * RANK), (2 * RANK) ** -0.5, 0.25, ((2, 16), (3, 16)))
    return dict(source=source, row_factors=row_factors, column_factors=column_factors)


def apply_level(coeffs, factors, stride):
    groups = coeffs.shape[0]
    middle = coeffs.shape[1]
    rank_size = coeffs.shape[2]
    rhs_count = coeffs.shape[3]
    paired = coeffs.reshape(groups // (2 * stride), 2, stride, middle, rank_size, rhs_count).astype(jnp.float32)
    mats = factors.reshape(groups // (2 * stride), 2, stride, middle, rank_size, 2 * rank_size).astype(jnp.float32)
    lower_part = paired[:, 0]
    upper_part = paired[:, 1]
    result = jnp.einsum('aqsmrk,asmkh->aqsmrh', mats[..., :rank_size], lower_part)
    result = result + jnp.einsum('aqsmrk,asmkh->aqsmrh', mats[..., rank_size:], upper_part)
    return result.reshape(groups, middle, rank_size, rhs_count).astype(jnp.bfloat16)


def reference(source, row_factors, column_factors):
    coeffs = source.reshape(BLK_DEV * LEAVES, STRIPS, RANK, RHS)
    forward = row_factors.reshape(LEVELS, BLK_DEV * LEAVES, STRIPS, RANK, 2 * RANK)
    for level_no in range(LEVELS):
        coeffs = apply_level(coeffs, forward[level_no], 2 ** level_no)
    coeffs = coeffs.reshape(BLK_DEV, LEAVES, STRIPS, RANK, RHS).transpose(0, 2, 1, 3, 4)
    coeffs = coeffs.reshape(BLK_DEV * STRIPS, LEAVES, RANK, RHS)
    adjoint = column_factors.transpose(0, 1, 3, 2, 4, 5).reshape(LEVELS, BLK_DEV * STRIPS, LEAVES, RANK, 2 * RANK)
    for level_no in reversed(range(LEVELS)):
        coeffs = apply_level(coeffs, adjoint[level_no], 2 ** level_no)
    coeffs = coeffs.reshape(BLK_DEV, STRIPS, LEAVES, RANK, RHS).transpose(0, 2, 1, 3, 4)
    return coeffs
```

```python
import functools

import jax
import jax.numpy as jnp
from jax import lax
from jax.experimental import pallas as pl
from jax.experimental.pallas import tpu as pltpu
from jax.sharding import PartitionSpec as P

WIDTHS = (512, 512)
RANK = 256
VMEM = 48 * 2**20


def swap_dest(step):
    pairs = []
    for device in range(256):
        leaf, wide = device >> 4, device & 15
        core, top, low = leaf & 1, wide >> 3, (wide >> 1) & 3
        dest_leaf = (leaf & ~1) | top
        dest_wide = (core << 3) | ((low ^ step) << 1) | (wide & 1)
        pairs.append((device, dest_leaf << 4 | dest_wide))
    return pairs


SWAPS = [swap_dest(step) for step in range(4)]


def swap(value, step):
    return lax.ppermute(value, ("leaf", "wide"), SWAPS[step])


def exchange(value, axis, mask):
    return lax.ppermute(value, axis, [(d, d ^ mask) for d in range(16)])


def dot(a, b):
    return jnp.dot(a, b, preferred_element_type=jnp.float32)


def cross(factor, own, other, high):
    first = pl.multiple_of(high * RANK, RANK)
    second = pl.multiple_of((1 - high) * RANK, RANK)
    total = dot(factor[:, pl.ds(first, RANK)], own) + dot(factor[:, pl.ds(second, RANK)], other)
    return total.astype(jnp.bfloat16)


def level_body(split, flags, factor, own, partner, *outs):
    high = flags[1]
    result = cross(factor.at[0, 0], own[0], partner[0], high)
    if split:
        for step in range(4):
            @pl.when(pl.program_id(0) == step)
            def _():
                outs[step][...] = result
    else:
        outs[-1][0] = result


def cost(n_dots, width, bytes_accessed):
    return pl.CostEstimate(flops=1, bytes_accessed=1, transcendentals=0)


def level_call(factors, level_no, own, partner, flags, width, natural=False, split=False, into=None, column=None, total_width=None, steps=(0, 1, 2, 3)):
    block = (1, RANK, width)
    stride, first = steps[1] - steps[0], steps[0]
    if natural:
        place = lambda t, s: (s[0] ^ t, 0, 0)
    else:
        place = lambda t, s: (t, 0, 0)
    in_specs = [
        pl.BlockSpec((1, 1, RANK, 2 * RANK), lambda t, s: (level_no, s[0] ^ (t * stride + first), 0, 0)),
        pl.BlockSpec(block, place),
        pl.BlockSpec(block, place),
    ]
    operands = [factors, own, partner]
    aliases = {}
    if split:
        out_shape = [jax.ShapeDtypeStruct((RANK, width), jnp.bfloat16)] * 4
        out_specs = [pl.BlockSpec((RANK, width), lambda t, s: (0, 0))] * 4
    elif column is not None:
        out_shape = jax.ShapeDtypeStruct((4, RANK, total_width), jnp.bfloat16)
        out_specs = pl.BlockSpec(block, lambda t, s: (s[0] ^ (t * stride + first), 0, column // width))
        if into is not None:
            in_specs.append(pl.BlockSpec(memory_space=pl.ANY))
            operands.append(into)
            aliases = {4: 0}
    else:
        out_shape = jax.ShapeDtypeStruct((4, RANK, width), jnp.bfloat16)
        out_specs = pl.BlockSpec(block, lambda t, s: (t, 0, 0))
    return pl.pallas_call(
        functools.partial(level_body, split),
        grid_spec=pltpu.PrefetchScalarGridSpec(num_scalar_prefetch=1, grid=(len(steps),), in_specs=in_specs, out_specs=out_specs),
        out_shape=out_shape,
        input_output_aliases=aliases,
        cost_estimate=cost(8, width, 4 * RANK * (3 * width + 2 * RANK) * 2),
        compiler_params=pltpu.CompilerParams(vmem_limit_bytes=VMEM),
    )(flags, *operands)


def take_body(flags, *refs):
    for t in range(4):
        for h in range(2):
            refs[4 + 2 * t + h][0] = refs[t][0, 0, h * (RANK // 2) : (h + 1) * (RANK // 2)]


def take_call(factors, flags):
    block = lambda step: pl.BlockSpec((1, 1, RANK, 2 * RANK), lambda g, s: (g + 1, s[0] ^ step, 0, 0))
    return pl.pallas_call(
        take_body,
        grid_spec=pltpu.PrefetchScalarGridSpec(
            num_scalar_prefetch=1,
            grid=(3,),
            in_specs=[block(t) for t in range(4)],
            out_specs=[pl.BlockSpec((1, RANK // 2, 2 * RANK), lambda g, s: (g, 0, 0))] * 8,
        ),
        out_shape=[jax.ShapeDtypeStruct((3, RANK // 2, 2 * RANK), jnp.bfloat16)] * 8,
        cost_estimate=cost(8, RANK, 1),
        compiler_params=pltpu.CompilerParams(vmem_limit_bytes=VMEM),
    )(flags, *[factors] * 4)


def three_body(flags, own, partner, *refs):
    low, high = flags[0], flags[1]
    factors, outs = refs[:8], refs[8:]

    def halves(t, row, mine, other, is_high):
        parts = [cross(factors[2 * t + h].at[row], mine, other, is_high) for h in range(2)]
        return jnp.concatenate(parts, axis=0)

    values = [halves(t, 2, own[t], partner[t], high) for t in range(4)]
    for bit, row in ((1, 1), (0, 0)):
        apart = 1 << bit
        values = [halves(t, row, values[t], values[t ^ apart], ((low ^ t) >> bit) & 1) for t in range(4)]
    for t in range(4):
        outs[t][...] = values[t]


def three_call(factors, own, partner, flags, width):
    whole = lambda shape: pl.BlockSpec(shape, lambda g, s: (0,) * len(shape))
    return pl.pallas_call(
        three_body,
        grid_spec=pltpu.PrefetchScalarGridSpec(
            num_scalar_prefetch=1,
            grid=(1,),
            in_specs=[whole((4, RANK, width))] * 2 + [whole((3, RANK // 2, 2 * RANK))] * 8,
            out_specs=[whole((RANK, width))] * 4,
        ),
        out_shape=[jax.ShapeDtypeStruct((RANK, width), jnp.bfloat16)] * 4,
        cost_estimate=cost(24, width, 4 * RANK * (3 * width + 6 * RANK) * 2),
        compiler_params=pltpu.CompilerParams(vmem_limit_bytes=VMEM),
    )(flags, own, partner, *factors)


GROUPS = ((1, 3), (0, 2))


def make_order():
    order = []
    work = lambda *name: order.append(("work", name))
    start = lambda *name: order.append(("start", name))
    done = lambda *name: order.append(("done", name))

    def level(number, chunk):
        done("send", number, chunk)
        work("level", number, chunk)

    def all_of(action, kind, chunk, steps=(1, 3, 0, 2)):
        for t in steps:
            action(kind, t, chunk)

    pieces = [(t, h) for h in range(2) for t in (1, 3, 0, 2)]
    batches = (pieces[:2], pieces[2:5], pieces[5:])

    def factor(batch, action):
        for piece in batches[batch]:
            action("fsend", *piece)

    work("cut", 0)
    start("send", 0, 0)
    work("fcut")
    factor(0, start)
    level(0, 0)
    start("send", 1, 0)
    work("cut", 1)
    start("send", 0, 1)
    level(0, 1)
    factor(0, done)
    factor(1, start)
    level(1, 0)
    start("send", 2, 0)
    start("send", 1, 1)
    factor(1, done)
    factor(2, start)
    level(2, 0)
    start("send", 3, 0)
    level(1, 1)
    factor(2, done)
    done("send", 3, 0)
    start("send", 2, 1)
    work("level", 3, 0)
    all_of(start, "go", 0)
    level(2, 1)
    start("send", 3, 1)
    all_of(done, "go", 0)
    start("acore", 0)
    done("acore", 0)
    work("three", 0)
    all_of(start, "back", 0)
    level(3, 1)
    all_of(done, "back", 0, GROUPS[0])
    all_of(start, "go", 1, GROUPS[0])
    start("dsend", 0, 0)
    all_of(done, "back", 0, GROUPS[1])
    all_of(start, "go", 1, GROUPS[1])
    done("dsend", 0, 0)
    start("dsend", 1, 0)
    work("last", 0, 0)
    all_of(done, "go", 1)
    start("acore", 1)
    done("dsend", 1, 0)
    work("last", 1, 0)
    done("acore", 1)
    work("three", 1)
    all_of(start, "back", 1)
    all_of(done, "back", 1, GROUPS[0])
    start("dsend", 0, 1)
    all_of(done, "back", 1, GROUPS[1])
    start("dsend", 1, 1)
    for h in range(2):
        done("dsend", h, 1)
        work("last", h, 1)
    return order


def per_device(source, row_factors, column_factors):
    columns = source.shape[-1]
    source = source.reshape(4, RANK, columns)
    forward = row_factors.reshape(4, 4, RANK, 2 * RANK)
    adjoint = column_factors.reshape(4, 4, RANK, 2 * RANK)
    leaf, wide = lax.axis_index("leaf"), lax.axis_index("wide")
    low = (wide >> 1) & 3
    row_flags = [jnp.stack([low, (leaf >> level) & 1]).astype(jnp.int32) for level in range(4)]
    last_flags = jnp.stack([low, wide & 1]).astype(jnp.int32)
    starts = [sum(WIDTHS[:c]) for c in range(len(WIDTHS))]

    order = make_order()
    values = {}
    token = last_flags
    output = None

    def tie(value):
        nonlocal token
        value, token = lax.optimization_barrier((value, token))
        return value

    for action, name in order:
        kind = name[0]
        if action == "done":
            values[name] = tie(values[name])
        elif action == "work":
            c = name[-1]
            if kind == "fcut":
                values[name] = tie(take_call(adjoint, tie(last_flags)))
            elif kind == "cut":
                block = lax.slice_in_dim(tie(source), starts[c], starts[c] + WIDTHS[c], axis=2)
                values[name] = tie(block)
            elif kind == "level":
                level = name[1]
                own = values["cut", c] if level == 0 else values["level", level - 1, c]
                result = level_call(
                    forward, level, tie(own), values["send", level, c], row_flags[level], WIDTHS[c],
                    natural=level == 0, split=level == 3,
                )
                values[name] = tie(result)
            elif kind == "three":
                result = three_call(
                    [values["fsend", t, h] for t in range(4) for h in range(2)], tie(values["stack", c]), values["acore", c], row_flags[0], WIDTHS[c],
                )
                values[name] = tie(result)
            elif kind == "last":
                half = name[1]
                output = level_call(
                    adjoint, 0, tie(values["dstack", half, c]), values["dsend", half, c], last_flags, WIDTHS[c],
                    into=output, column=starts[c], total_width=columns, steps=GROUPS[half],
                )
                output = tie(output)
        else:
            c = name[-1]
            if kind == "fsend":
                values[name] = swap(tie(values["fcut",][2 * name[1] + c]), name[1])
            elif kind == "send":
                level = name[1]
                own = values["cut", c] if level == 0 else values["level", level - 1, c]
                values[name] = exchange(tie(own), "leaf", 1 << level)
            elif kind == "go":
                values[name] = swap(tie(values["level", 3, c][name[1]]), name[1])
            elif kind == "acore":
                values["stack", c] = tie(jnp.stack([values["go", t, c] for t in range(4)]))
                values[name] = exchange(values["stack", c], "leaf", 1)
            elif kind == "back":
                values[name] = swap(tie(values["three", c][name[1]]), name[1])
            elif kind == "dsend":
                half = name[1]
                stack = tie(jnp.stack([values["back", t, c] for t in GROUPS[half]]))
                values["dstack", half, c] = stack
                values[name] = exchange(stack, "wide", 1)
    return output.reshape(4, 1, 1, RANK, columns)


def solution(mesh):
    return jax.shard_map(
        per_device,
        mesh=mesh,
        in_specs=(
            P(None, "leaf", "wide", None, None),
            P(None, None, "leaf", "wide", None, None),
            P(None, None, "leaf", "wide", None, None),
        ),
        out_specs=P(None, "leaf", "wide", None, None),
        check_vma=False,
    )
```

```python
import functools

import jax
import jax.numpy as jnp
from jax import lax
from jax.experimental import pallas as pl
from jax.experimental.pallas import tpu as pltpu
from jax.sharding import PartitionSpec as P

WIDTHS = (512, 512)
RANK = 256
VMEM = 48 * 2**20


def swap_dest(step):
    pairs = []
    for device in range(256):
        leaf, wide = device >> 4, device & 15
        core, top, low = leaf & 1, wide >> 3, (wide >> 1) & 3
        dest_leaf = (leaf & ~1) | top
        dest_wide = (core << 3) | ((low ^ step) << 1) | (wide & 1)
        pairs.append((device, dest_leaf << 4 | dest_wide))
    return pairs


SWAPS = [swap_dest(step) for step in range(4)]


def swap(value, step):
    return lax.ppermute(value, ("leaf", "wide"), SWAPS[step])


def exchange(value, axis, mask):
    return lax.ppermute(value, axis, [(d, d ^ mask) for d in range(16)])


def dot(a, b):
    return jnp.dot(a, b, preferred_element_type=jnp.float32)


def cross(factor, own, other, high):
    first = pl.multiple_of(high * RANK, RANK)
    second = pl.multiple_of((1 - high) * RANK, RANK)
    total = dot(factor[:, pl.ds(first, RANK)], own) + dot(factor[:, pl.ds(second, RANK)], other)
    return total.astype(jnp.bfloat16)


def level_body(split, flags, factor, own, partner, *outs):
    high = flags[1]
    result = cross(factor.at[0, 0], own[0], partner[0], high)
    if split:
        for place in range(2):
            @pl.when(pl.program_id(0) == place)
            def _():
                outs[place][...] = result
    else:
        outs[-1][0] = result


def cost(n_dots, width, bytes_accessed):
    return pl.CostEstimate(flops=1, bytes_accessed=1, transcendentals=0)


def level_call(factors, level_no, own, partner, flags, width, natural=False, split=False, into=None, column=None, total_width=None, steps=(0, 1, 2, 3)):
    block = (1, RANK, width)
    stride, first = steps[1] - steps[0], steps[0]
    if natural:
        place = lambda t, s: (s[0] ^ (t * stride + first), 0, 0)
    else:
        place = lambda t, s: (t, 0, 0)
    in_specs = [
        pl.BlockSpec((1, 1, RANK, 2 * RANK), lambda t, s: (level_no, s[0] ^ (t * stride + first), 0, 0)),
        pl.BlockSpec(block, place),
        pl.BlockSpec(block, place),
    ]
    operands = [factors, own, partner]
    aliases = {}
    if split:
        out_shape = [jax.ShapeDtypeStruct((RANK, width), jnp.bfloat16)] * 2
        out_specs = [pl.BlockSpec((RANK, width), lambda t, s: (0, 0))] * 2
    elif column is not None:
        out_shape = jax.ShapeDtypeStruct((4, RANK, total_width), jnp.bfloat16)
        out_specs = pl.BlockSpec(block, lambda t, s: (s[0] ^ (t * stride + first), 0, column // width))
        if into is not None:
            in_specs.append(pl.BlockSpec(memory_space=pl.ANY))
            operands.append(into)
            aliases = {4: 0}
    else:
        out_shape = jax.ShapeDtypeStruct((len(steps), RANK, width), jnp.bfloat16)
        out_specs = pl.BlockSpec(block, lambda t, s: (t, 0, 0))
    return pl.pallas_call(
        functools.partial(level_body, split),
        grid_spec=pltpu.PrefetchScalarGridSpec(num_scalar_prefetch=1, grid=(len(steps),), in_specs=in_specs, out_specs=out_specs),
        out_shape=out_shape,
        input_output_aliases=aliases,
        cost_estimate=cost(8, width, 4 * RANK * (3 * width + 2 * RANK) * 2),
        compiler_params=pltpu.CompilerParams(vmem_limit_bytes=VMEM),
    )(flags, *operands)


def take_body(flags, *refs):
    for t in range(4):
        refs[4 + t][0] = refs[t][0, 0]


def take_call(factors, flags):
    block = lambda step: pl.BlockSpec((1, 1, RANK, 2 * RANK), lambda g, s: (g + 1, s[0] ^ step, 0, 0))
    return pl.pallas_call(
        take_body,
        grid_spec=pltpu.PrefetchScalarGridSpec(
            num_scalar_prefetch=1,
            grid=(3,),
            in_specs=[block(t) for t in range(4)],
            out_specs=[pl.BlockSpec((1, RANK, 2 * RANK), lambda g, s: (g, 0, 0))] * 4,
        ),
        out_shape=[jax.ShapeDtypeStruct((3, RANK, 2 * RANK), jnp.bfloat16)] * 4,
        cost_estimate=cost(8, RANK, 1),
        compiler_params=pltpu.CompilerParams(vmem_limit_bytes=VMEM),
    )(flags, *[factors] * 4)


def three_body(flags, own, partner, *refs):
    low, high = flags[0], flags[1]
    factors, outs = refs[:4], refs[4:]
    values = [cross(factors[t].at[2], own[t], partner[t], high) for t in range(4)]
    for bit, row in ((1, 1), (0, 0)):
        apart = 1 << bit
        values = [
            cross(factors[t].at[row], values[t], values[t ^ apart], ((low ^ t) >> bit) & 1) for t in range(4)
        ]
    for t in range(4):
        outs[t][...] = values[t]


def three_call(factors, own, partner, flags, width):
    whole = lambda shape: pl.BlockSpec(shape, lambda g, s: (0,) * len(shape))
    return pl.pallas_call(
        three_body,
        grid_spec=pltpu.PrefetchScalarGridSpec(
            num_scalar_prefetch=1,
            grid=(1,),
            in_specs=[whole((4, RANK, width))] * 2 + [whole((3, RANK, 2 * RANK))] * 4,
            out_specs=[whole((RANK, width))] * 4,
        ),
        out_shape=[jax.ShapeDtypeStruct((RANK, width), jnp.bfloat16)] * 4,
        cost_estimate=cost(24, width, 4 * RANK * (3 * width + 6 * RANK) * 2),
        compiler_params=pltpu.CompilerParams(vmem_limit_bytes=VMEM),
    )(flags, own, partner, *factors)


GROUPS = ((0, 2), (1, 3))


class Order(list):
    def work(self, *name):
        self.append(("work", name))

    def start(self, *name):
        self.append(("start", name))

    def done(self, *name):
        self.append(("done", name))

    def level(self, number, u):
        if number:
            self.done("send", number, u % 2, u // 2)
        self.work("level", number, u % 2, u // 2)

    def send(self, number, u):
        self.start("send", number, u % 2, u // 2)


def order_before():
    o = Order()
    o.work("cut", 0)
    o.start("core", 0)
    o.work("fcut")
    o.work("cut", 1)
    o.start("core", 1)
    o.done("core", 0)
    o.done("core", 1)
    o.start("fsend", 0)
    o.start("fsend", 1)
    o.start("fsend", 2)
    return o


def order_region():
    o = Order()
    o.level(0, 0)
    o.send(1, 0)
    o.level(0, 1)
    o.send(1, 1)
    o.level(0, 2)
    o.level(0, 3)
    o.level(1, 0)
    o.send(2, 0)
    o.level(1, 1)
    o.send(2, 1)
    o.level(2, 0)
    o.send(3, 0)
    o.level(2, 1)
    o.send(1, 2)
    o.done("send", 3, 0, 0)
    o.send(3, 1)
    o.work("level", 3, 0, 0)
    o.level(1, 2)
    o.send(1, 3)
    o.level(3, 1)
    o.level(1, 3)
    return o


def order_after():
    o = Order()
    o.send(2, 2)
    o.send(2, 3)
    o.start("fsend", 3)
    o.start("go", 0, 0)
    o.start("go", 2, 0)
    o.done("fsend", 0)
    o.done("fsend", 1)
    o.done("fsend", 2)
    o.level(2, 2)
    o.send(3, 2)
    o.done("fsend", 3)
    o.start("go", 1, 0)
    o.done("go", 2, 0)
    o.start("go", 3, 0)
    o.level(2, 3)
    o.send(3, 3)
    o.done("go", 0, 0)
    o.level(3, 2)
    o.start("go", 0, 1)
    o.done("go", 1, 0)
    o.start("go", 2, 1)
    o.level(3, 3)
    o.start("go", 1, 1)
    o.done("go", 3, 0)
    o.start("go", 3, 1)
    o.start("acore", 0)
    o.done("acore", 0)
    o.work("three", 0)
    o.done("go", 2, 1)
    o.start("back", 0, 0)
    o.done("go", 0, 1)
    o.start("back", 2, 0)
    o.done("go", 1, 1)
    o.start("back", 1, 0)
    o.done("go", 3, 1)
    o.start("back", 3, 0)
    o.start("acore", 1)
    o.done("back", 2, 0)
    o.done("back", 0, 0)
    o.start("dsend", 0, 0)
    o.done("acore", 1)
    o.work("three", 1)
    o.start("back", 0, 1)
    o.start("back", 2, 1)
    o.done("back", 1, 0)
    o.done("back", 3, 0)
    o.start("dsend", 1, 0)
    o.start("back", 1, 1)
    o.start("back", 3, 1)
    o.done("dsend", 0, 0)
    o.work("last", 0, 0)
    o.done("back", 2, 1)
    o.done("back", 0, 1)
    o.start("dsend", 0, 1)
    o.done("dsend", 1, 0)
    o.work("last", 1, 0)
    o.done("back", 1, 1)
    o.done("back", 3, 1)
    o.start("dsend", 1, 1)
    for h in range(2):
        o.done("dsend", h, 1)
        o.work("last", h, 1)
    return o


def region(function, *operands):
    shapes = jax.eval_shape(function, *operands)
    empty = lambda *_: jax.tree.map(lambda s: jnp.zeros(s.shape, s.dtype), shapes)
    return lax.cond(lax.axis_index("leaf") < 16, function, empty, *operands)


def per_device(source, row_factors, column_factors):
    columns = source.shape[-1]
    source = source.reshape(4, RANK, columns)
    forward = row_factors.reshape(4, 4, RANK, 2 * RANK)
    adjoint = column_factors.reshape(4, 4, RANK, 2 * RANK)
    leaf, wide = lax.axis_index("leaf"), lax.axis_index("wide")
    low = (wide >> 1) & 3
    row_flags = [jnp.stack([low, (leaf >> level) & 1]).astype(jnp.int32) for level in range(4)]
    last_flags = jnp.stack([low, wide & 1]).astype(jnp.int32)
    starts = [sum(WIDTHS[:c]) for c in range(len(WIDTHS))]

    values = {}
    token = last_flags
    output = None

    def tie(value):
        nonlocal token
        value, token = lax.optimization_barrier((value, token))
        return value

    def run(order):
        for action, name in order:
            step(action, name)

    def step(action, name):
        nonlocal output
        kind = name[0]
        if action == "done":
            values[name] = tie(values[name])
        elif action == "work":
            c = name[-1]
            if kind == "fcut":
                values[name] = tie(take_call(adjoint, tie(last_flags)))
            elif kind == "cut":
                block = lax.slice_in_dim(tie(source), starts[c], starts[c] + WIDTHS[c], axis=2)
                values[name] = tie(block)
            elif kind == "level":
                level, g = name[1:3]
                own = values["cut", c] if level == 0 else values["level", level - 1, g, c]
                partner = values["core", c] if level == 0 else values["send", level, g, c]
                result = level_call(
                    forward, level, tie(own), partner, row_flags[level], WIDTHS[c],
                    natural=level == 0, split=level == 3, steps=GROUPS[g],
                )
                values[name] = tie(result)
            elif kind == "three":
                result = three_call(
                    [values["fsend", t] for t in range(4)], tie(values["stack", c]), values["acore", c], row_flags[0], WIDTHS[c],
                )
                values[name] = tie(result)
            elif kind == "last":
                half = name[1]
                output = level_call(
                    adjoint, 0, tie(values["dstack", half, c]), values["dsend", half, c], last_flags, WIDTHS[c],
                    into=output, column=starts[c], total_width=columns, steps=GROUPS[half],
                )
                output = tie(output)
        else:
            c = name[-1]
            if kind == "fsend":
                values[name] = swap(tie(values["fcut",][c]), c)
            elif kind == "core":
                values[name] = exchange(tie(values["cut", c]), "leaf", 1)
            elif kind == "send":
                level, g = name[1:3]
                values[name] = exchange(tie(values["level", level - 1, g, c]), "leaf", 1 << level)
            elif kind == "go":
                g = name[1] % 2
                values[name] = swap(tie(values["level", 3, g, c][GROUPS[g].index(name[1])]), name[1])
            elif kind == "acore":
                values["stack", c] = tie(jnp.stack([values["go", t, c] for t in range(4)]))
                values[name] = exchange(values["stack", c], "leaf", 1)
            elif kind == "back":
                values[name] = swap(tie(values["three", c][name[1]]), name[1])
            elif kind == "dsend":
                half = name[1]
                stack = tie(jnp.stack([values["back", t, c] for t in GROUPS[half]]))
                values["dstack", half, c] = stack
                values[name] = exchange(stack, "wide", 1)
    run(order_before())
    keep = [("level", 3, g, 0) for g in range(2)] + [("level", 1, g, 1) for g in range(2)]

    def body(first):
        nonlocal token
        token = first
        run(order_region())
        return [values[name] for name in keep], token

    kept, token = region(body, token)
    values.update(zip(keep, kept))
    run(order_after())
    return output.reshape(4, 1, 1, RANK, columns)


def solution(mesh):
    return jax.shard_map(
        per_device,
        mesh=mesh,
        in_specs=(
            P(None, "leaf", "wide", None, None),
            P(None, None, "leaf", "wide", None, None),
            P(None, None, "leaf", "wide", None, None),
        ),
        out_specs=P(None, "leaf", "wide", None, None),
        check_vma=False,
    )
```

```python
import functools

import jax
import jax.numpy as jnp
from jax import lax
from jax.experimental import pallas as pl
from jax.experimental.pallas import tpu as pltpu
from jax.sharding import PartitionSpec as P

WIDTHS = (512, 512)
RANK = 256
VMEM = 48 * 2**20


def swap_dest(step):
    pairs = []
    for device in range(256):
        leaf, wide = device >> 4, device & 15
        core, top, low = leaf & 1, wide >> 3, (wide >> 1) & 3
        dest_leaf = (leaf & ~1) | top
        dest_wide = (core << 3) | ((low ^ step) << 1) | (wide & 1)
        pairs.append((device, dest_leaf << 4 | dest_wide))
    return pairs


SWAPS = [swap_dest(step) for step in range(4)]


def swap(value, step):
    return lax.ppermute(value, ("leaf", "wide"), SWAPS[step])


def exchange(value, axis, mask):
    return lax.ppermute(value, axis, [(d, d ^ mask) for d in range(16)])


def dot(a, b):
    return jnp.dot(a, b, preferred_element_type=jnp.float32)


def cross(factor, own, other, high):
    first = pl.multiple_of(high * RANK, RANK)
    second = pl.multiple_of((1 - high) * RANK, RANK)
    total = dot(factor[:, pl.ds(first, RANK)], own) + dot(factor[:, pl.ds(second, RANK)], other)
    return total.astype(jnp.bfloat16)


def level_body(split, flags, factor, own, partner, *outs):
    high = flags[1]
    result = cross(factor.at[0, 0], own[0], partner[0], high)
    if split:
        for place in range(2):
            @pl.when(pl.program_id(0) == place)
            def _():
                outs[place][...] = result
    else:
        outs[-1][0] = result


def cost(n_dots, width, bytes_accessed):
    return pl.CostEstimate(flops=1, bytes_accessed=1, transcendentals=0)


def level_call(factors, level_no, own, partner, flags, width, natural=False, split=False, into=None, column=None, total_width=None, steps=(0, 1, 2, 3)):
    block = (1, RANK, width)
    stride, first = steps[1] - steps[0], steps[0]
    if natural:
        place = lambda t, s: (s[0] ^ (t * stride + first), 0, 0)
    else:
        place = lambda t, s: (t, 0, 0)
    in_specs = [
        pl.BlockSpec((1, 1, RANK, 2 * RANK), lambda t, s: (level_no, s[0] ^ (t * stride + first), 0, 0)),
        pl.BlockSpec(block, place),
        pl.BlockSpec(block, place),
    ]
    operands = [factors, own, partner]
    aliases = {}
    if split:
        out_shape = [jax.ShapeDtypeStruct((RANK, width), jnp.bfloat16)] * 2
        out_specs = [pl.BlockSpec((RANK, width), lambda t, s: (0, 0))] * 2
    elif column is not None:
        out_shape = jax.ShapeDtypeStruct((4, RANK, total_width), jnp.bfloat16)
        out_specs = pl.BlockSpec(block, lambda t, s: (s[0] ^ (t * stride + first), 0, column // width))
        if into is not None:
            in_specs.append(pl.BlockSpec(memory_space=pl.ANY))
            operands.append(into)
            aliases = {4: 0}
    else:
        out_shape = jax.ShapeDtypeStruct((len(steps), RANK, width), jnp.bfloat16)
        out_specs = pl.BlockSpec(block, lambda t, s: (t, 0, 0))
    return pl.pallas_call(
        functools.partial(level_body, split),
        grid_spec=pltpu.PrefetchScalarGridSpec(num_scalar_prefetch=1, grid=(len(steps),), in_specs=in_specs, out_specs=out_specs),
        out_shape=out_shape,
        input_output_aliases=aliases,
        cost_estimate=cost(8, width, 4 * RANK * (3 * width + 2 * RANK) * 2),
        compiler_params=pltpu.CompilerParams(vmem_limit_bytes=VMEM),
    )(flags, *operands)


def take_body(flags, *refs):
    for t in range(4):
        refs[4 + t][0] = refs[t][0, 0]


def take_call(factors, flags):
    block = lambda step: pl.BlockSpec((1, 1, RANK, 2 * RANK), lambda g, s: (g + 1, s[0] ^ step, 0, 0))
    return pl.pallas_call(
        take_body,
        grid_spec=pltpu.PrefetchScalarGridSpec(
            num_scalar_prefetch=1,
            grid=(3,),
            in_specs=[block(t) for t in range(4)],
            out_specs=[pl.BlockSpec((1, RANK, 2 * RANK), lambda g, s: (g, 0, 0))] * 4,
        ),
        out_shape=[jax.ShapeDtypeStruct((3, RANK, 2 * RANK), jnp.bfloat16)] * 4,
        cost_estimate=cost(8, RANK, 1),
        compiler_params=pltpu.CompilerParams(vmem_limit_bytes=VMEM),
    )(flags, *[factors] * 4)


def three_body(flags, own, partner, *refs):
    low, high = flags[0], flags[1]
    factors, outs = refs[:4], refs[4:]
    values = [cross(factors[t].at[2], own[t], partner[t], high) for t in range(4)]
    for bit, row in ((1, 1), (0, 0)):
        apart = 1 << bit
        values = [
            cross(factors[t].at[row], values[t], values[t ^ apart], ((low ^ t) >> bit) & 1) for t in range(4)
        ]
    for t in range(4):
        outs[t][...] = values[t]


def three_call(factors, own, partner, flags, width):
    whole = lambda shape: pl.BlockSpec(shape, lambda g, s: (0,) * len(shape))
    return pl.pallas_call(
        three_body,
        grid_spec=pltpu.PrefetchScalarGridSpec(
            num_scalar_prefetch=1,
            grid=(1,),
            in_specs=[whole((4, RANK, width))] * 2 + [whole((3, RANK, 2 * RANK))] * 4,
            out_specs=[whole((RANK, width))] * 4,
        ),
        out_shape=[jax.ShapeDtypeStruct((RANK, width), jnp.bfloat16)] * 4,
        cost_estimate=cost(24, width, 4 * RANK * (3 * width + 6 * RANK) * 2),
        compiler_params=pltpu.CompilerParams(vmem_limit_bytes=VMEM),
    )(flags, own, partner, *factors)


GROUPS = ((0, 2), (1, 3))


class Order(list):
    def work(self, *name):
        self.append(("work", name))

    def start(self, *name):
        self.append(("start", name))

    def done(self, *name):
        self.append(("done", name))

    def level(self, number, u):
        if number:
            self.done("send", number, u % 2, u // 2)
        self.work("level", number, u % 2, u // 2)

    def send(self, number, u):
        self.start("send", number, u % 2, u // 2)


def order_before():
    o = Order()
    o.work("cut", 0)
    o.start("core", 0)
    o.work("fcut")
    o.work("cut", 1)
    o.start("core", 1)
    o.done("core", 0)
    o.done("core", 1)
    o.start("fsend", 0)
    o.start("fsend", 1)
    o.start("fsend", 2)
    return o


def order_region():
    o = Order()
    o.level(0, 0)
    o.send(1, 0)
    o.level(0, 1)
    o.send(1, 1)
    o.level(0, 2)
    o.level(0, 3)
    o.level(1, 0)
    o.send(2, 0)
    o.level(1, 1)
    o.send(2, 1)
    o.level(2, 0)
    o.send(3, 0)
    o.level(2, 1)
    o.send(1, 2)
    o.done("send", 3, 0, 0)
    o.send(3, 1)
    o.work("level", 3, 0, 0)
    o.level(1, 2)
    o.send(1, 3)
    o.level(3, 1)
    o.level(1, 3)
    return o


def order_after():
    o = Order()
    o.send(2, 2)
    o.send(2, 3)
    o.start("fsend", 3)
    o.start("go", 0, 0)
    o.start("go", 2, 0)
    o.done("fsend", 0)
    o.done("fsend", 1)
    o.done("fsend", 2)
    o.level(2, 2)
    o.send(3, 2)
    o.done("fsend", 3)
    o.start("go", 1, 0)
    o.done("go", 2, 0)
    o.start("go", 3, 0)
    o.level(2, 3)
    o.send(3, 3)
    o.done("go", 0, 0)
    o.level(3, 2)
    o.start("go", 0, 1)
    o.done("go", 1, 0)
    o.start("go", 2, 1)
    o.level(3, 3)
    o.start("go", 1, 1)
    o.done("go", 3, 0)
    o.start("go", 3, 1)
    o.start("acore", 0)
    o.done("acore", 0)
    o.work("three", 0)
    o.start("back", 0, 0)
    o.done("go", 2, 1)
    o.start("back", 2, 0)
    o.done("go", 0, 1)
    o.done("go", 1, 1)
    o.start("back", 1, 0)
    o.done("go", 3, 1)
    o.done("back", 2, 0)
    o.start("back", 3, 0)
    o.done("back", 0, 0)
    o.start("dsend", 0, 0)
    o.start("acore", 1)
    o.done("acore", 1)
    o.work("three", 1)
    o.start("back", 0, 1)
    o.start("back", 2, 1)
    o.done("back", 1, 0)
    o.done("back", 3, 0)
    o.start("dsend", 1, 0)
    o.start("back", 1, 1)
    o.start("back", 3, 1)
    o.done("dsend", 0, 0)
    o.work("last", 0, 0)
    o.done("back", 2, 1)
    o.done("back", 0, 1)
    o.start("dsend", 0, 1)
    o.done("dsend", 1, 0)
    o.work("last", 1, 0)
    o.done("back", 1, 1)
    o.done("back", 3, 1)
    o.start("dsend", 1, 1)
    for h in range(2):
        o.done("dsend", h, 1)
        o.work("last", h, 1)
    return o


def region(function, *operands):
    shapes = jax.eval_shape(function, *operands)
    empty = lambda *_: jax.tree.map(lambda s: jnp.zeros(s.shape, s.dtype), shapes)
    return lax.cond(lax.axis_index("leaf") < 16, function, empty, *operands)


def per_device(source, row_factors, column_factors):
    columns = source.shape[-1]
    source = source.reshape(4, RANK, columns)
    forward = row_factors.reshape(4, 4, RANK, 2 * RANK)
    adjoint = column_factors.reshape(4, 4, RANK, 2 * RANK)
    leaf, wide = lax.axis_index("leaf"), lax.axis_index("wide")
    low = (wide >> 1) & 3
    row_flags = [jnp.stack([low, (leaf >> level) & 1]).astype(jnp.int32) for level in range(4)]
    last_flags = jnp.stack([low, wide & 1]).astype(jnp.int32)
    starts = [sum(WIDTHS[:c]) for c in range(len(WIDTHS))]

    values = {}
    token = last_flags
    output = None

    def tie(value):
        nonlocal token
        value, token = lax.optimization_barrier((value, token))
        return value

    def run(order):
        for action, name in order:
            step(action, name)

    def step(action, name):
        nonlocal output
        kind = name[0]
        if action == "done":
            values[name] = tie(values[name])
        elif action == "work":
            c = name[-1]
            if kind == "fcut":
                values[name] = tie(take_call(adjoint, tie(last_flags)))
            elif kind == "cut":
                block = lax.slice_in_dim(tie(source), starts[c], starts[c] + WIDTHS[c], axis=2)
                values[name] = tie(block)
            elif kind == "level":
                level, g = name[1:3]
                own = values["cut", c] if level == 0 else values["level", level - 1, g, c]
                partner = values["core", c] if level == 0 else values["send", level, g, c]
                result = level_call(
                    forward, level, tie(own), partner, row_flags[level], WIDTHS[c],
                    natural=level == 0, split=level == 3, steps=GROUPS[g],
                )
                values[name] = tie(result)
            elif kind == "three":
                result = three_call(
                    [values["fsend", t] for t in range(4)], tie(values["stack", c]), values["acore", c], row_flags[0], WIDTHS[c],
                )
                values[name] = tie(result)
            elif kind == "last":
                half = name[1]
                output = level_call(
                    adjoint, 0, tie(values["dstack", half, c]), values["dsend", half, c], last_flags, WIDTHS[c],
                    into=output, column=starts[c], total_width=columns, steps=GROUPS[half],
                )
                output = tie(output)
        else:
            c = name[-1]
            if kind == "fsend":
                values[name] = swap(tie(values["fcut",][c]), c)
            elif kind == "core":
                values[name] = exchange(tie(values["cut", c]), "leaf", 1)
            elif kind == "send":
                level, g = name[1:3]
                values[name] = exchange(tie(values["level", level - 1, g, c]), "leaf", 1 << level)
            elif kind == "go":
                g = name[1] % 2
                values[name] = swap(tie(values["level", 3, g, c][GROUPS[g].index(name[1])]), name[1])
            elif kind == "acore":
                values["stack", c] = tie(jnp.stack([values["go", t, c] for t in range(4)]))
                values[name] = exchange(values["stack", c], "leaf", 1)
            elif kind == "back":
                values[name] = swap(tie(values["three", c][name[1]]), name[1])
            elif kind == "dsend":
                half = name[1]
                stack = tie(jnp.stack([values["back", t, c] for t in GROUPS[half]]))
                values["dstack", half, c] = stack
                values[name] = exchange(stack, "wide", 1)
    run(order_before())
    keep = [("level", 3, g, 0) for g in range(2)] + [("level", 1, g, 1) for g in range(2)]

    def body(first):
        nonlocal token
        token = first
        run(order_region())
        return [values[name] for name in keep], token

    kept, token = region(body, token)
    values.update(zip(keep, kept))
    run(order_after())
    return output.reshape(4, 1, 1, RANK, columns)


def solution(mesh):
    return jax.shard_map(
        per_device,
        mesh=mesh,
        in_specs=(
            P(None, "leaf", "wide", None, None),
            P(None, None, "leaf", "wide", None, None),
            P(None, None, "leaf", "wide", None, None),
        ),
        out_specs=P(None, "leaf", "wide", None, None),
        check_vma=False,
    )
```

```python
import functools

import jax
import jax.numpy as jnp
from jax import lax
from jax.experimental import pallas as pl
from jax.experimental.pallas import tpu as pltpu
from jax.sharding import PartitionSpec as P

WIDTHS = (512, 512)
RANK = 256
VMEM = 16 * 2**20


def swap_dest(step):
    pairs = []
    for device in range(256):
        leaf, wide = device >> 4, device & 15
        core, top, low = leaf & 1, wide >> 3, (wide >> 1) & 3
        dest_leaf = (leaf & ~1) | top
        dest_wide = (core << 3) | ((low ^ step) << 1) | (wide & 1)
        pairs.append((device, dest_leaf << 4 | dest_wide))
    return pairs


SWAPS = [swap_dest(step) for step in range(4)]


def swap(value, step):
    return lax.ppermute(value, ("leaf", "wide"), SWAPS[step])


def exchange(value, axis, mask):
    return lax.ppermute(value, axis, [(d, d ^ mask) for d in range(16)])


def dot(a, b):
    return jnp.dot(a, b, preferred_element_type=jnp.float32)


def cross(factor, own, other, high):
    first = pl.multiple_of(high * RANK, RANK)
    second = pl.multiple_of((1 - high) * RANK, RANK)
    total = dot(factor[:, pl.ds(first, RANK)], own) + dot(factor[:, pl.ds(second, RANK)], other)
    return total.astype(jnp.bfloat16)


def level_body(split, flags, factor, own, partner, *outs):
    high = flags[1]
    result = cross(factor.at[0, 0], own[0], partner[0], high)
    if split:
        for place in range(2):
            @pl.when(pl.program_id(0) == place)
            def _():
                outs[place][...] = result
    else:
        outs[-1][0] = result


def cost(n_dots, width, bytes_accessed):
    return pl.CostEstimate(flops=1, bytes_accessed=1, transcendentals=0)


def level_call(factors, level_no, own, partner, flags, width, natural=False, split=False, into=None, column=None, total_width=None, steps=(0, 1, 2, 3)):
    block = (1, RANK, width)
    stride, first = steps[1] - steps[0], steps[0]
    if natural:
        place = lambda t, s: (s[0] ^ (t * stride + first), 0, 0)
    else:
        place = lambda t, s: (t, 0, 0)
    in_specs = [
        pl.BlockSpec((1, 1, RANK, 2 * RANK), lambda t, s: (level_no, s[0] ^ (t * stride + first), 0, 0)),
        pl.BlockSpec(block, place),
        pl.BlockSpec(block, place),
    ]
    operands = [factors, own, partner]
    aliases = {}
    if split:
        out_shape = [jax.ShapeDtypeStruct((RANK, width), jnp.bfloat16)] * 2
        out_specs = [pl.BlockSpec((RANK, width), lambda t, s: (0, 0))] * 2
    elif column is not None:
        out_shape = jax.ShapeDtypeStruct((4, RANK, total_width), jnp.bfloat16)
        out_specs = pl.BlockSpec(block, lambda t, s: (s[0] ^ (t * stride + first), 0, column // width))
        if into is not None:
            in_specs.append(pl.BlockSpec(memory_space=pl.ANY))
            operands.append(into)
            aliases = {4: 0}
    else:
        out_shape = jax.ShapeDtypeStruct((len(steps), RANK, width), jnp.bfloat16)
        out_specs = pl.BlockSpec(block, lambda t, s: (t, 0, 0))
    return pl.pallas_call(
        functools.partial(level_body, split),
        grid_spec=pltpu.PrefetchScalarGridSpec(num_scalar_prefetch=1, grid=(len(steps),), in_specs=in_specs, out_specs=out_specs),
        out_shape=out_shape,
        input_output_aliases=aliases,
        cost_estimate=cost(8, width, 4 * RANK * (3 * width + 2 * RANK) * 2),
        compiler_params=pltpu.CompilerParams(vmem_limit_bytes=VMEM),
    )(flags, *operands)


def take_body(flags, *refs):
    for t in range(4):
        refs[4 + t][0] = refs[t][0, 0]


def take_call(factors, flags):
    block = lambda step: pl.BlockSpec((1, 1, RANK, 2 * RANK), lambda g, s: (g + 1, s[0] ^ step, 0, 0))
    return pl.pallas_call(
        take_body,
        grid_spec=pltpu.PrefetchScalarGridSpec(
            num_scalar_prefetch=1,
            grid=(3,),
            in_specs=[block(t) for t in range(4)],
            out_specs=[pl.BlockSpec((1, RANK, 2 * RANK), lambda g, s: (g, 0, 0))] * 4,
        ),
        out_shape=[jax.ShapeDtypeStruct((3, RANK, 2 * RANK), jnp.bfloat16)] * 4,
        cost_estimate=cost(8, RANK, 1),
        compiler_params=pltpu.CompilerParams(vmem_limit_bytes=VMEM),
    )(flags, *[factors] * 4)


def three_body(flags, own, partner, *refs):
    low, high = flags[0], flags[1]
    factors, outs = refs[:4], refs[4:]
    values = [cross(factors[t].at[2], own[t], partner[t], high) for t in range(4)]
    for bit, row in ((1, 1), (0, 0)):
        apart = 1 << bit
        values = [
            cross(factors[t].at[row], values[t], values[t ^ apart], ((low ^ t) >> bit) & 1) for t in range(4)
        ]
    for t in range(4):
        outs[t][...] = values[t]


def three_call(factors, own, partner, flags, width):
    whole = lambda shape: pl.BlockSpec(shape, lambda g, s: (0,) * len(shape))
    return pl.pallas_call(
        three_body,
        grid_spec=pltpu.PrefetchScalarGridSpec(
            num_scalar_prefetch=1,
            grid=(1,),
            in_specs=[whole((4, RANK, width))] * 2 + [whole((3, RANK, 2 * RANK))] * 4,
            out_specs=[whole((RANK, width))] * 4,
        ),
        out_shape=[jax.ShapeDtypeStruct((RANK, width), jnp.bfloat16)] * 4,
        cost_estimate=cost(24, width, 4 * RANK * (3 * width + 6 * RANK) * 2),
        compiler_params=pltpu.CompilerParams(vmem_limit_bytes=VMEM),
    )(flags, own, partner, *factors)


GROUPS = ((0, 2), (1, 3))


class Order(list):
    def work(self, *name):
        self.append(("work", name))

    def start(self, *name):
        self.append(("start", name))

    def done(self, *name):
        self.append(("done", name))

    def level(self, number, u):
        if number:
            self.done("send", number, u % 2, u // 2)
        self.work("level", number, u % 2, u // 2)

    def send(self, number, u):
        self.start("send", number, u % 2, u // 2)


def order_before():
    o = Order()
    o.work("cut", 0)
    o.start("core", 0)
    o.work("fcut")
    o.work("cut", 1)
    o.start("core", 1)
    o.done("core", 0)
    o.done("core", 1)
    o.start("fsend", 0)
    o.start("fsend", 1)
    o.start("fsend", 2)
    return o


def order_region():
    o = Order()
    o.level(0, 0)
    o.send(1, 0)
    o.level(0, 1)
    o.send(1, 1)
    o.level(0, 2)
    o.level(0, 3)
    o.level(1, 0)
    o.send(2, 0)
    o.level(1, 1)
    o.send(2, 1)
    o.level(2, 0)
    o.send(3, 0)
    o.level(2, 1)
    o.send(1, 2)
    o.done("send", 3, 0, 0)
    o.send(3, 1)
    o.work("level", 3, 0, 0)
    o.level(1, 2)
    o.send(1, 3)
    o.level(3, 1)
    o.level(1, 3)
    return o


def order_after():
    o = Order()
    o.send(2, 2)
    o.send(2, 3)
    o.start("fsend", 3)
    o.start("go", 0, 0)
    o.start("go", 2, 0)
    o.done("fsend", 0)
    o.done("fsend", 1)
    o.done("fsend", 2)
    o.level(2, 2)
    o.send(3, 2)
    o.done("fsend", 3)
    o.start("go", 1, 0)
    o.done("go", 2, 0)
    o.start("go", 3, 0)
    o.level(2, 3)
    o.send(3, 3)
    o.done("go", 0, 0)
    o.level(3, 2)
    o.start("go", 0, 1)
    o.done("go", 1, 0)
    o.start("go", 2, 1)
    o.level(3, 3)
    o.start("go", 1, 1)
    o.done("go", 3, 0)
    o.start("go", 3, 1)
    o.start("acore", 0)
    o.done("acore", 0)
    o.work("three", 0)
    o.start("back", 0, 0)
    o.done("go", 2, 1)
    o.start("back", 2, 0)
    o.done("go", 0, 1)
    o.done("go", 1, 1)
    o.start("back", 1, 0)
    o.done("go", 3, 1)
    o.done("back", 2, 0)
    o.start("back", 3, 0)
    o.done("back", 0, 0)
    o.start("dsend", 0, 0)
    o.start("acore", 1)
    o.done("acore", 1)
    o.work("three", 1)
    o.start("back", 0, 1)
    o.start("back", 2, 1)
    o.done("back", 1, 0)
    o.done("back", 3, 0)
    o.start("dsend", 1, 0)
    o.start("back", 1, 1)
    o.start("back", 3, 1)
    o.done("dsend", 0, 0)
    o.work("last", 0, 0)
    o.done("back", 2, 1)
    o.done("back", 0, 1)
    o.start("dsend", 0, 1)
    o.done("dsend", 1, 0)
    o.work("last", 1, 0)
    o.done("back", 1, 1)
    o.done("back", 3, 1)
    o.start("dsend", 1, 1)
    for h in range(2):
        o.done("dsend", h, 1)
        o.work("last", h, 1)
    return o


def region(function, *operands):
    shapes = jax.eval_shape(function, *operands)
    empty = lambda *_: jax.tree.map(lambda s: jnp.zeros(s.shape, s.dtype), shapes)
    return lax.cond(lax.axis_index("leaf") < 16, function, empty, *operands)


def per_device(source, row_factors, column_factors):
    columns = source.shape[-1]
    source = source.reshape(4, RANK, columns)
    forward = row_factors.reshape(4, 4, RANK, 2 * RANK)
    adjoint = column_factors.reshape(4, 4, RANK, 2 * RANK)
    leaf, wide = lax.axis_index("leaf"), lax.axis_index("wide")
    low = (wide >> 1) & 3
    row_flags = [jnp.stack([low, (leaf >> level) & 1]).astype(jnp.int32) for level in range(4)]
    last_flags = jnp.stack([low, wide & 1]).astype(jnp.int32)
    starts = [sum(WIDTHS[:c]) for c in range(len(WIDTHS))]

    values = {}
    token = last_flags
    output = None

    def tie(value):
        nonlocal token
        value, token = lax.optimization_barrier((value, token))
        return value

    def run(order):
        for action, name in order:
            step(action, name)

    def step(action, name):
        nonlocal output
        kind = name[0]
        if action == "done":
            values[name] = tie(values[name])
        elif action == "work":
            c = name[-1]
            if kind == "fcut":
                values[name] = tie(take_call(adjoint, tie(last_flags)))
            elif kind == "cut":
                block = lax.slice_in_dim(tie(source), starts[c], starts[c] + WIDTHS[c], axis=2)
                values[name] = tie(block)
            elif kind == "level":
                level, g = name[1:3]
                own = values["cut", c] if level == 0 else values["level", level - 1, g, c]
                partner = values["core", c] if level == 0 else values["send", level, g, c]
                result = level_call(
                    forward, level, tie(own), partner, row_flags[level], WIDTHS[c],
                    natural=level == 0, split=level == 3, steps=GROUPS[g],
                )
                values[name] = tie(result)
            elif kind == "three":
                result = three_call(
                    [values["fsend", t] for t in range(4)], tie(values["stack", c]), values["acore", c], row_flags[0], WIDTHS[c],
                )
                values[name] = tie(result)
            elif kind == "last":
                half = name[1]
                output = level_call(
                    adjoint, 0, tie(values["dstack", half, c]), values["dsend", half, c], last_flags, WIDTHS[c],
                    into=output, column=starts[c], total_width=columns, steps=GROUPS[half],
                )
                output = tie(output)
        else:
            c = name[-1]
            if kind == "fsend":
                values[name] = swap(tie(values["fcut",][c]), c)
            elif kind == "core":
                values[name] = exchange(tie(values["cut", c]), "leaf", 1)
            elif kind == "send":
                level, g = name[1:3]
                values[name] = exchange(tie(values["level", level - 1, g, c]), "leaf", 1 << level)
            elif kind == "go":
                g = name[1] % 2
                values[name] = swap(tie(values["level", 3, g, c][GROUPS[g].index(name[1])]), name[1])
            elif kind == "acore":
                values["stack", c] = tie(jnp.stack([values["go", t, c] for t in range(4)]))
                values[name] = exchange(values["stack", c], "leaf", 1)
            elif kind == "back":
                values[name] = swap(tie(values["three", c][name[1]]), name[1])
            elif kind == "dsend":
                half = name[1]
                stack = tie(jnp.stack([values["back", t, c] for t in GROUPS[half]]))
                values["dstack", half, c] = stack
                values[name] = exchange(stack, "wide", 1)
    run(order_before())
    keep = [("level", 3, g, 0) for g in range(2)] + [("level", 1, g, 1) for g in range(2)]

    def body(first):
        nonlocal token
        token = first
        run(order_region())
        return [values[name] for name in keep], token

    kept, token = region(body, token)
    values.update(zip(keep, kept))
    run(order_after())
    return output.reshape(4, 1, 1, RANK, columns)


def solution(mesh):
    return jax.shard_map(
        per_device,
        mesh=mesh,
        in_specs=(
            P(None, "leaf", "wide", None, None),
            P(None, None, "leaf", "wide", None, None),
            P(None, None, "leaf", "wide", None, None),
        ),
        out_specs=P(None, "leaf", "wide", None, None),
        check_vma=False,
    )
```

```python
import functools

import jax
import jax.numpy as jnp
from jax import lax
from jax.experimental import pallas as pl
from jax.experimental.pallas import tpu as pltpu
from jax.sharding import PartitionSpec as P

WIDTHS = (512, 512)
RANK = 256
VMEM = 16 * 2**20


def swap_dest(step):
    pairs = []
    for device in range(256):
        leaf, wide = device >> 4, device & 15
        core, top, low = leaf & 1, wide >> 3, (wide >> 1) & 3
        dest_leaf = (leaf & ~1) | top
        dest_wide = (core << 3) | ((low ^ step) << 1) | (wide & 1)
        pairs.append((device, dest_leaf << 4 | dest_wide))
    return pairs


SWAPS = [swap_dest(step) for step in range(4)]


def swap(value, step):
    return lax.ppermute(value, ("leaf", "wide"), SWAPS[step])


def exchange(value, axis, mask):
    return lax.ppermute(value, axis, [(d, d ^ mask) for d in range(16)])


def dot(a, b):
    return jnp.dot(a, b, preferred_element_type=jnp.float32)


def cross(factor, own, other, high):
    first = pl.multiple_of(high * RANK, RANK)
    second = pl.multiple_of((1 - high) * RANK, RANK)
    total = dot(factor[:, pl.ds(first, RANK)], own) + dot(factor[:, pl.ds(second, RANK)], other)
    return total.astype(jnp.bfloat16)


def level_body(split, flags, factor, own, partner, *outs):
    high = flags[1]
    result = cross(factor.at[0, 0], own[0], partner[0], high)
    if split:
        for place in range(2):
            @pl.when(pl.program_id(0) == place)
            def _():
                outs[place][...] = result
    else:
        outs[-1][0] = result


def cost(n_dots, width, bytes_accessed):
    return pl.CostEstimate(flops=1, bytes_accessed=1, transcendentals=0)


def level_call(factors, level_no, own, partner, flags, width, natural=False, split=False, into=None, column=None, total_width=None, steps=(0, 1, 2, 3)):
    block = (1, RANK, width)
    stride, first = steps[1] - steps[0], steps[0]
    if natural:
        place = lambda t, s: (s[0] ^ (t * stride + first), 0, 0)
    else:
        place = lambda t, s: (t, 0, 0)
    in_specs = [
        pl.BlockSpec((1, 1, RANK, 2 * RANK), lambda t, s: (level_no, s[0] ^ (t * stride + first), 0, 0)),
        pl.BlockSpec(block, place),
        pl.BlockSpec(block, place),
    ]
    operands = [factors, own, partner]
    aliases = {}
    if split:
        out_shape = [jax.ShapeDtypeStruct((RANK, width), jnp.bfloat16)] * 2
        out_specs = [pl.BlockSpec((RANK, width), lambda t, s: (0, 0))] * 2
    elif column is not None:
        out_shape = jax.ShapeDtypeStruct((4, RANK, total_width), jnp.bfloat16)
        out_specs = pl.BlockSpec(block, lambda t, s: (s[0] ^ (t * stride + first), 0, column // width))
        if into is not None:
            in_specs.append(pl.BlockSpec(memory_space=pl.ANY))
            operands.append(into)
            aliases = {4: 0}
    else:
        out_shape = jax.ShapeDtypeStruct((len(steps), RANK, width), jnp.bfloat16)
        out_specs = pl.BlockSpec(block, lambda t, s: (t, 0, 0))
    return pl.pallas_call(
        functools.partial(level_body, split),
        grid_spec=pltpu.PrefetchScalarGridSpec(num_scalar_prefetch=1, grid=(len(steps),), in_specs=in_specs, out_specs=out_specs),
        out_shape=out_shape,
        input_output_aliases=aliases,
        cost_estimate=cost(8, width, 4 * RANK * (3 * width + 2 * RANK) * 2),
        compiler_params=pltpu.CompilerParams(vmem_limit_bytes=VMEM),
    )(flags, *operands)


def take_body(flags, *refs):
    for t in range(4):
        refs[4 + t][0] = refs[t][0, 0]


def take_call(factors, flags):
    block = lambda step: pl.BlockSpec((1, 1, RANK, 2 * RANK), lambda g, s: (g + 1, s[0] ^ step, 0, 0))
    return pl.pallas_call(
        take_body,
        grid_spec=pltpu.PrefetchScalarGridSpec(
            num_scalar_prefetch=1,
            grid=(3,),
            in_specs=[block(t) for t in range(4)],
            out_specs=[pl.BlockSpec((1, RANK, 2 * RANK), lambda g, s: (g, 0, 0))] * 4,
        ),
        out_shape=[jax.ShapeDtypeStruct((3, RANK, 2 * RANK), jnp.bfloat16)] * 4,
        cost_estimate=cost(8, RANK, 1),
        compiler_params=pltpu.CompilerParams(vmem_limit_bytes=VMEM),
    )(flags, *[factors] * 4)


def three_body(flags, own, partner, *refs):
    low, high = flags[0], flags[1]
    factors, outs = refs[:4], refs[4:]
    values = [cross(factors[t].at[2], own[t], partner[t], high) for t in range(4)]
    for bit, row in ((1, 1), (0, 0)):
        apart = 1 << bit
        values = [
            cross(factors[t].at[row], values[t], values[t ^ apart], ((low ^ t) >> bit) & 1) for t in range(4)
        ]
    for t in range(4):
        outs[t][...] = values[t]


def three_call(factors, own, partner, flags, width):
    whole = lambda shape: pl.BlockSpec(shape, lambda g, s: (0,) * len(shape))
    return pl.pallas_call(
        three_body,
        grid_spec=pltpu.PrefetchScalarGridSpec(
            num_scalar_prefetch=1,
            grid=(1,),
            in_specs=[whole((4, RANK, width))] * 2 + [whole((3, RANK, 2 * RANK))] * 4,
            out_specs=[whole((RANK, width))] * 4,
        ),
        out_shape=[jax.ShapeDtypeStruct((RANK, width), jnp.bfloat16)] * 4,
        cost_estimate=cost(24, width, 4 * RANK * (3 * width + 6 * RANK) * 2),
        compiler_params=pltpu.CompilerParams(vmem_limit_bytes=VMEM),
    )(flags, own, partner, *factors)


GROUPS = ((0, 2), (1, 3))


class Order(list):
    def work(self, *name):
        self.append(("work", name))

    def start(self, *name):
        self.append(("start", name))

    def done(self, *name):
        self.append(("done", name))

    def level(self, number, u):
        if number:
            self.done("send", number, u % 2, u // 2)
        self.work("level", number, u % 2, u // 2)

    def send(self, number, u):
        self.start("send", number, u % 2, u // 2)


def order_before():
    o = Order()
    o.work("cut", 0)
    o.start("core", 0)
    o.work("fcut")
    o.work("cut", 1)
    o.start("core", 1)
    o.done("core", 0)
    o.done("core", 1)
    o.start("fsend", 0)
    o.start("fsend", 1)
    o.start("fsend", 2)
    return o


def order_region():
    o = Order()
    o.level(0, 0)
    o.send(1, 0)
    o.level(0, 1)
    o.send(1, 1)
    o.level(0, 2)
    o.level(0, 3)
    o.level(1, 0)
    o.send(2, 0)
    o.level(1, 1)
    o.send(2, 1)
    o.level(2, 0)
    o.send(3, 0)
    o.level(2, 1)
    o.send(1, 2)
    o.done("send", 3, 0, 0)
    o.send(3, 1)
    o.work("level", 3, 0, 0)
    o.level(1, 2)
    o.send(1, 3)
    o.level(3, 1)
    o.level(1, 3)
    return o


def order_after():
    o = Order()
    o.send(2, 2)
    o.send(2, 3)
    o.start("fsend", 3)
    o.start("go", 0, 0)
    o.start("go", 2, 0)
    o.done("fsend", 0)
    o.done("fsend", 1)
    o.done("fsend", 2)
    o.level(2, 2)
    o.send(3, 2)
    o.done("fsend", 3)
    o.start("go", 1, 0)
    o.done("go", 2, 0)
    o.start("go", 3, 0)
    o.level(2, 3)
    o.send(3, 3)
    o.done("go", 0, 0)
    o.level(3, 2)
    o.start("go", 0, 1)
    o.done("go", 1, 0)
    o.start("go", 2, 1)
    o.level(3, 3)
    o.start("go", 1, 1)
    o.done("go", 3, 0)
    o.start("go", 3, 1)
    o.start("acore", 0)
    o.done("acore", 0)
    o.work("three", 0)
    o.start("back", 0, 0)
    o.done("go", 2, 1)
    o.start("back", 2, 0)
    o.done("go", 0, 1)
    o.done("go", 1, 1)
    o.start("back", 1, 0)
    o.done("go", 3, 1)
    o.done("back", 2, 0)
    o.start("back", 3, 0)
    o.done("back", 0, 0)
    o.start("dsend", 0, 0)
    o.start("acore", 1)
    o.done("acore", 1)
    o.work("three", 1)
    o.start("back", 0, 1)
    o.start("back", 2, 1)
    o.done("back", 1, 0)
    o.done("back", 3, 0)
    o.start("dsend", 1, 0)
    o.done("dsend", 0, 0)
    o.work("last", 0, 0)
    o.start("back", 1, 1)
    o.start("back", 3, 1)
    o.done("back", 2, 1)
    o.done("back", 0, 1)
    o.start("dsend", 0, 1)
    o.done("dsend", 1, 0)
    o.work("last", 1, 0)
    o.done("back", 1, 1)
    o.done("back", 3, 1)
    o.start("dsend", 1, 1)
    for h in range(2):
        o.done("dsend", h, 1)
        o.work("last", h, 1)
    return o


def region(function, *operands):
    shapes = jax.eval_shape(function, *operands)
    empty = lambda *_: jax.tree.map(lambda s: jnp.zeros(s.shape, s.dtype), shapes)
    return lax.cond(lax.axis_index("leaf") < 16, function, empty, *operands)


def per_device(source, row_factors, column_factors):
    columns = source.shape[-1]
    source = source.reshape(4, RANK, columns)
    forward = row_factors.reshape(4, 4, RANK, 2 * RANK)
    adjoint = column_factors.reshape(4, 4, RANK, 2 * RANK)
    leaf, wide = lax.axis_index("leaf"), lax.axis_index("wide")
    low = (wide >> 1) & 3
    row_flags = [jnp.stack([low, (leaf >> level) & 1]).astype(jnp.int32) for level in range(4)]
    last_flags = jnp.stack([low, wide & 1]).astype(jnp.int32)
    starts = [sum(WIDTHS[:c]) for c in range(len(WIDTHS))]

    values = {}
    token = last_flags
    output = None

    def tie(value):
        nonlocal token
        value, token = lax.optimization_barrier((value, token))
        return value

    def run(order):
        for action, name in order:
            step(action, name)

    def step(action, name):
        nonlocal output
        kind = name[0]
        if action == "done":
            values[name] = tie(values[name])
        elif action == "work":
            c = name[-1]
            if kind == "fcut":
                values[name] = tie(take_call(adjoint, tie(last_flags)))
            elif kind == "cut":
                block = lax.slice_in_dim(tie(source), starts[c], starts[c] + WIDTHS[c], axis=2)
                values[name] = tie(block)
            elif kind == "level":
                level, g = name[1:3]
                own = values["cut", c] if level == 0 else values["level", level - 1, g, c]
                partner = values["core", c] if level == 0 else values["send", level, g, c]
                result = level_call(
                    forward, level, tie(own), partner, row_flags[level], WIDTHS[c],
                    natural=level == 0, split=level == 3, steps=GROUPS[g],
                )
                values[name] = tie(result)
            elif kind == "three":
                result = three_call(
                    [values["fsend", t] for t in range(4)], tie(values["stack", c]), values["acore", c], row_flags[0], WIDTHS[c],
                )
                values[name] = tie(result)
            elif kind == "last":
                half = name[1]
                output = level_call(
                    adjoint, 0, tie(values["dstack", half, c]), values["dsend", half, c], last_flags, WIDTHS[c],
                    into=output, column=starts[c], total_width=columns, steps=GROUPS[half],
                )
                output = tie(output)
        else:
            c = name[-1]
            if kind == "fsend":
                values[name] = swap(tie(values["fcut",][c]), c)
            elif kind == "core":
                values[name] = exchange(tie(values["cut", c]), "leaf", 1)
            elif kind == "send":
                level, g = name[1:3]
                values[name] = exchange(tie(values["level", level - 1, g, c]), "leaf", 1 << level)
            elif kind == "go":
                g = name[1] % 2
                values[name] = swap(tie(values["level", 3, g, c][GROUPS[g].index(name[1])]), name[1])
            elif kind == "acore":
                values["stack", c] = tie(jnp.stack([values["go", t, c] for t in range(4)]))
                values[name] = exchange(values["stack", c], "leaf", 1)
            elif kind == "back":
                values[name] = swap(tie(values["three", c][name[1]]), name[1])
            elif kind == "dsend":
                half = name[1]
                stack = tie(jnp.stack([values["back", t, c] for t in GROUPS[half]]))
                values["dstack", half, c] = stack
                values[name] = exchange(stack, "wide", 1)
    run(order_before())
    keep = [("level", 3, g, 0) for g in range(2)] + [("level", 1, g, 1) for g in range(2)]

    def body(first):
        nonlocal token
        token = first
        run(order_region())
        return [values[name] for name in keep], token

    kept, token = region(body, token)
    values.update(zip(keep, kept))
    run(order_after())
    return output.reshape(4, 1, 1, RANK, columns)


def solution(mesh):
    return jax.shard_map(
        per_device,
        mesh=mesh,
        in_specs=(
            P(None, "leaf", "wide", None, None),
            P(None, None, "leaf", "wide", None, None),
            P(None, None, "leaf", "wide", None, None),
        ),
        out_specs=P(None, "leaf", "wide", None, None),
        check_vma=False,
    )
```
